256 devices in a mesh: store: 16 (over z_lo, y), ctx: 16 (over x, z_hi, core).
Axes of the slice: x: 4, y: 4, z: 8 (z_hi: 2, z_lo: 4; z = z_hi * 4 + z_lo), core: 2. Of those that a mesh axis runs over, the one named last changes fastest.
Arguments:
- queries: bfloat16 [16384, 4096], P(('store', 'ctx')), may hold values from -24 to 24
- question_kv: bfloat16 [16384, 1024], P(('store', 'ctx')), may hold values from -6 to 6
- passage_kv: bfloat16 [2048, 64, 1024], P(('store', 'ctx')), may hold values from -6 to 6
- wanted: int32 [16, 16, 8], P(None, 'ctx'), may hold values from 0 to 2047, as said below
- live: int32 [16, 16], P(None, 'ctx'), may hold values from 6 to 8, as said below
Outputs:
- attended: bfloat16 [16384, 4096], P(('store', 'ctx'))
The draws below stay inside these ranges and needn't reach their ends.
Inputs may be any that keep to these rules, and one draw needn't show every extreme that they name: Entry wanted[s, c, j] is stored on the device with store index wanted[s, c, j] // 128 and ctx index c; the 8 entries of one (s, c) lie on different store shards. Entries j < live[s, c] of wanted[s, c] are read, the others are not. In every request group some device reads all 8.
All inputs are finite; a program needn't handle non-finite values.
Results may differ from the reference program's by a relative error of at most 0.0038.
Values may be sent and summed in bfloat16 or wider, within the bound.
No kernel may reach another device: no remote copies, remote signals or barrier semaphores. Data moves between devices by JAX's collectives and lax.ppermute only.
A program may use at most 192 MiB of HBM per device.

```python
import math
import jax
import jax.numpy as jnp
from jax import lax

HQ = 32
KVH = 4
HD = 128
BLK = 64
SB = 8
GROUPS = 16
LOCAL = 8
SPLITS = 16
QLEN = 1024


def draw_queries(key, part):
    key = jax.random.fold_in(key, 11)
    shape = (GROUPS * QLEN, HQ * HD)
    values = jnp.clip(2.0 * jax.random.normal(key, shape, jnp.float32), -12.0, 12.0)
    return values.astype(jnp.bfloat16)


def draw_passage_kv(key, part):
    key = jax.random.fold_in(key, 23)
    shape = (GROUPS * SPLITS * SB, BLK, 2 * KVH * HD)
    first_key = jax.random.fold_in(key, 0)
    values = jnp.clip(jax.random.normal(first_key, shape, jnp.float32), -6.0, 6.0)
    return values.astype(jnp.bfloat16)


def draw_wanted(key, part):
    key = jax.random.fold_in(key, 37)
    pair_count = GROUPS * SPLITS
    first_key, second_key = jax.random.split(key)
    pair_keys = jax.random.split(first_key, pair_count)
    stores = jax.vmap(lambda one_key: jax.random.permutation(one_key, GROUPS)[:LOCAL])(pair_keys).astype(jnp.int32)
    slots = jax.random.randint(second_key, (pair_count, LOCAL), 0, SB, dtype=jnp.int32)
    column = lax.broadcasted_iota(jnp.int32, (pair_count, 1), 0) % SPLITS
    block_ids = (stores * SPLITS + column) * SB + slots
    return block_ids.reshape(GROUPS, SPLITS, LOCAL).astype(jnp.int32)


def draw_live(key, part):
    key = jax.random.fold_in(key, 53)
    first_key, second_key, third_key = jax.random.split(key, 3)
    lowest = max(2, LOCAL - 2)
    first_count = jax.random.randint(first_key, (GROUPS, SPLITS), lowest, LOCAL + 1, dtype=jnp.int32)
    second_count = jax.random.randint(second_key, (GROUPS, SPLITS), lowest, LOCAL + 1, dtype=jnp.int32)
    counts = jnp.maximum(first_count, second_count)
    full_device = jax.random.randint(third_key, (GROUPS, 1), 0, SPLITS, dtype=jnp.int32)
    columns = lax.broadcasted_iota(jnp.int32, (GROUPS, SPLITS), 1)
    return jnp.where(columns == full_device, LOCAL, counts).astype(jnp.int32)


def shard_levels(stream_key, dims, cuts, least, largest):
    gain, own = 1.0, jax.random.fold_in(stream_key, 6)
    for position, blocks in cuts:
        heights = jnp.exp(jax.random.uniform(jax.random.fold_in(own, position), (blocks,), jnp.float32, least / len(cuts), largest / len(cuts)))
        gain = gain * jnp.repeat(heights, dims[position] // blocks).reshape([-1 if axis == position else 1 for axis in range(len(dims))])
    return gain


def centred(key, dims, scale, most, cuts=(), kind=jnp.bfloat16):
    values = scale * jax.random.normal(key, dims, jnp.float32)
    if cuts:
        values = values * shard_levels(key, dims, cuts, -0.22, 0.18)
    return jnp.clip(values, -most, most).astype(kind)


def setup_inputs(seed: int = 0) -> dict:
    key_list = jax.random.split(jax.random.key(seed), 6)
    queries = draw_queries(jax.random.fold_in(key_list[5], 71), 0)
    question_kv = centred(key_list[1], (GROUPS * QLEN, 2 * KVH * HD), 1.0, 6.0, ((0, 256),))
    passage_kv = draw_passage_kv(jax.random.fold_in(key_list[5], 71), 0)
    wanted = draw_wanted(jax.random.fold_in(key_list[5], 71), 0)
    live = draw_live(jax.random.fold_in(key_list[5], 71), 0)
    return {"queries": queries, "question_kv": question_kv, "passage_kv": passage_kv, "wanted": wanted, "live": live}


def reference(queries, question_kv, passage_kv, wanted, live):
    per_group = HQ // KVH
    kv_width = KVH * HD
    score_scale = 1.0 / math.sqrt(HD)

    def one_group(group_index):
        row_start = (group_index * QLEN).astype(jnp.int32)
        query_rows = lax.dynamic_slice_in_dim(queries, row_start, QLEN, 0).astype(jnp.float32)
        own_keys = lax.dynamic_slice_in_dim(question_kv, row_start, QLEN, 0).astype(jnp.float32)
        block_ids = lax.dynamic_index_in_dim(wanted, group_index, 0, keepdims=False).reshape(-1).astype(jnp.int32)
        counts = lax.dynamic_index_in_dim(live, group_index, 0, keepdims=False)
        block_rows = jnp.take(passage_kv, block_ids, axis=0).astype(jnp.float32).reshape(SPLITS * LOCAL * BLK, 2 * kv_width)
        live_mask = lax.broadcasted_iota(jnp.int32, (SPLITS, LOCAL, BLK), 1) < counts[:, None, None]
        key_flags = live_mask.reshape(-1)
        positions = lax.broadcasted_iota(jnp.int32, (QLEN,), 0)
        causal = positions[None, :] <= positions[:, None]
        visible = jnp.concatenate([jnp.broadcast_to(key_flags[None, :], (QLEN, key_flags.shape[0])), causal], axis=1)
        keys_all = jnp.concatenate([block_rows, own_keys], axis=0)
        head_outputs = []
        for kv_head in range(KVH):
            query_head = query_rows[:, kv_head * per_group * HD:(kv_head + 1) * per_group * HD].reshape(QLEN, per_group, HD)
            key_head = keys_all[:, kv_head * HD:(kv_head + 1) * HD]
            value_head = keys_all[:, kv_width + kv_head * HD:kv_width + (kv_head + 1) * HD]
            scores = jnp.einsum('qpd,kd->qpk', query_head, key_head) * score_scale
            scores = jnp.where(visible[:, None, :], scores, -1e+30)
            row_max = lax.optimization_barrier(jnp.max(scores, axis=2, keepdims=True))
            weights = jnp.exp(scores - row_max)
            row_total = lax.optimization_barrier(jnp.sum(weights, axis=2, keepdims=True))
            rounded = lax.optimization_barrier(weights.astype(jnp.bfloat16)).astype(jnp.float32)
            head_outputs.append(jnp.einsum('qpk,kd->qpd', rounded, value_head) / row_total)
        return jnp.concatenate(head_outputs, axis=1).reshape(QLEN, HQ * HD).astype(jnp.bfloat16)
    result = lax.map(one_group, jnp.arange(GROUPS, dtype=jnp.int32))
    return result.reshape(GROUPS * QLEN, HQ * HD)
```

```python
import functools
import math

import jax
import jax.numpy as jnp
from jax import lax
from jax.experimental import pallas as pl
from jax.experimental.pallas import tpu as pltpu
from jax.sharding import Mesh, PartitionSpec as P

HQ = 32
KVH = 4
HD = 128
GROUP_HEADS = HQ // KVH
BLK = 64
GROUPS = 16
LOCAL = 8
STORED = 8
ROWS = 64
INFO_ROWS = 16
PIECE_ROWS = ROWS + INFO_ROWS
QCOLS = GROUP_HEADS * HD
PIECE = QCOLS + 2 * HD
HEAD_ROWS = 4 * ROWS
ALL_ROWS = GROUP_HEADS * HEAD_ROWS
STEP_HEADS = 2
STEP_ROWS = STEP_HEADS * HEAD_ROWS
EXP2_SCALE = math.log2(math.e) / math.sqrt(HD)
LOWEST = -1e30
CHUNKS = (48, 16)
KEY_TILE = 1024

AXES = ("zlo", "y", "x", "zhi", "core")
HEAD_AXES = ("zhi", "core")
SEND_AXES = ("zlo", "y", "zhi", "core")

VMEM = pl.BlockSpec(memory_space=pltpu.VMEM)
SMEM = pl.BlockSpec(memory_space=pltpu.SMEM)
BF16 = jnp.bfloat16


def params(mib=40):
    return pltpu.CompilerParams(vmem_limit_bytes=mib * 2**20)


def cost(flops, size):
    return pl.CostEstimate(flops=flops, bytes_accessed=size, transcendentals=0)


def bf16_shape(*dims):
    return jax.ShapeDtypeStruct(dims, BF16)


def columns(index, width):
    return pl.ds(pl.multiple_of(index * width, width), width)


def split_kernel(head_ref, q_ref, kv_ref, info_ref, *outs):
    for offset, out in enumerate(outs):
        head = head_ref[0] ^ offset
        out[:ROWS, :QCOLS] = q_ref[:, columns(head, QCOLS)]
        out[ROWS:, :QCOLS] = jnp.zeros((INFO_ROWS, QCOLS), BF16)
        out[:ROWS, QCOLS : QCOLS + HD] = kv_ref[:, columns(head, HD)]
        out[:ROWS, QCOLS + HD :] = kv_ref[:, columns(KVH + head, HD)]
        out[ROWS:, QCOLS:] = info_ref[...]


def split_queries(head, queries, question_kv, info):
    return pl.pallas_call(
        split_kernel,
        out_shape=[bf16_shape(PIECE_ROWS, PIECE)] * 4,
        in_specs=[SMEM, VMEM, VMEM, VMEM],
        out_specs=[VMEM] * 4,
        compiler_params=params(16),
        cost_estimate=cost(0, 1 << 20),
    )(head, queries, question_kv, info)


def select_kernel(slot_ref, stored_ref, *outs):
    def one(group, carry):
        slot = slot_ref[group]
        start = 0
        for size, out in zip(CHUNKS, outs):
            tokens = slice(start, start + size)
            for head in range(KVH):
                keys = slice(head * HD, (head + 1) * HD)
                values = slice((KVH + head) * HD, (KVH + head + 1) * HD)
                out[group * KVH + head, :, :HD] = stored_ref[slot, tokens, keys]
                out[group * KVH + head, :, HD:] = stored_ref[slot, tokens, values]
            start += size
        return carry

    lax.fori_loop(0, GROUPS, one, 0)


def select_blocks(slots, stored):
    return pl.pallas_call(
        select_kernel,
        out_shape=[bf16_shape(GROUPS * KVH, size, 2 * HD) for size in CHUNKS],
        in_specs=[SMEM, VMEM],
        out_specs=[VMEM] * len(CHUNKS),
        compiler_params=params(16),
        cost_estimate=cost(0, 3 << 20),
    )(slots, stored)


def collect_kernel(p0, p1, p2, p3, question, info):
    for offset, piece in enumerate((p0, p1, p2, p3)):
        rows = slice(offset * PIECE_ROWS, (offset + 1) * PIECE_ROWS)
        question[rows, :] = piece[:, QCOLS:]
        told = piece[ROWS:, QCOLS:].astype(jnp.float32)
        info[offset : offset + 1, :] = told[:1, :].astype(jnp.int32)


def collect(pieces):
    return pl.pallas_call(
        collect_kernel,
        out_shape=[
            bf16_shape(4 * PIECE_ROWS, 2 * HD),
            jax.ShapeDtypeStruct((4, 2 * HD), jnp.int32),
        ],
        in_specs=[VMEM] * 4,
        out_specs=[VMEM] * 2,
        compiler_params=params(16),
        cost_estimate=cost(0, 1 << 20),
    )(*pieces)


def pack_kernel(slot_ref, flag_ref, landed_ref, out_ref):
    tokens = landed_ref.shape[1]

    def one(entry, carry):
        rows = columns(entry, tokens)
        out_ref[rows, :] = landed_ref[slot_ref[entry]]

        @pl.when(flag_ref[entry] == 0)
        def _():
            out_ref[rows, HD:] = jnp.zeros((tokens, HD), BF16)

        return carry

    lax.fori_loop(0, 4 * LOCAL, one, 0)


def pack_blocks(slots, flags, landed):
    tokens = landed.shape[1]
    return pl.pallas_call(
        pack_kernel,
        out_shape=bf16_shape(4 * LOCAL * tokens, 2 * HD),
        in_specs=[SMEM, SMEM, VMEM],
        out_specs=VMEM,
        compiler_params=params(16),
        cost_estimate=cost(0, 3 << 20),
    )(slots, flags, landed)


def step(query, keys, values, state_max, state_sum, mask=None):
    scores = lax.dot_general(
        query, keys, (((1,), (1,)), ((), ())), preferred_element_type=jnp.float32
    )
    if mask is not None:
        scores = jnp.where(mask, scores, LOWEST)
    new_max = jnp.maximum(state_max, jnp.max(scores, axis=1, keepdims=True))
    scale = jnp.exp2((state_max - new_max) * EXP2_SCALE)
    weights = jnp.exp2((scores - new_max[:, :1]) * EXP2_SCALE).astype(jnp.bfloat16)
    summed = jnp.dot(weights, values, preferred_element_type=jnp.float32)
    return new_max, state_sum * jnp.concatenate([scale, scale], axis=1) + summed


def question_kernel(
    place_ref, p0, p1, p2, p3, left, right, far, q_out, max_out, sum_out, flag_out, held
):
    head, column = place_ref[0], place_ref[1]
    ones = jnp.ones((HEAD_ROWS, HD), BF16)
    entry = lax.broadcasted_iota(jnp.int32, (LOCAL, HD), 0).astype(jnp.float32)

    def hold(slot, offset, piece, row, start):
        held[slot, offset * ROWS : (offset + 1) * ROWS, :] = piece[row : row + ROWS, start:]
        info = piece[row + ROWS : row + PIECE_ROWS, start + HD :].astype(jnp.float32)
        first = (slot * 4 + offset) * LOCAL
        flag_out[first : first + LOCAL, :] = (entry < info[:1, :]).astype(jnp.float32)

    for offset, piece in enumerate((p0, p1, p2, p3)):
        hold(0, offset, piece, 0, QCOLS)
        for h in range(GROUP_HEADS):
            start = h * HEAD_ROWS + offset * ROWS
            q_out[start : start + ROWS, :] = piece[:ROWS, h * HD : (h + 1) * HD]
        for slot, other in enumerate((left, right, far)):
            hold(slot + 1, offset, other, offset * PIECE_ROWS, 0)

    def positions(axis, shape):
        index = lax.broadcasted_iota(jnp.int32, shape, axis)
        return ((index // ROWS) ^ head) * ROWS + index % ROWS

    shape = (HEAD_ROWS, HEAD_ROWS)
    mask = positions(1, shape) <= positions(0, shape)
    low = jnp.full((HEAD_ROWS, HD), LOWEST, jnp.float32)
    zero = jnp.zeros((HEAD_ROWS, 2 * HD), jnp.float32)

    def first(h, carry):
        rows = columns(h, HEAD_ROWS)
        values = jnp.concatenate([held[0, :, HD:], ones], axis=1)
        max_out[rows, :], sum_out[rows, :] = step(
            q_out[rows, :], held[0, :, :HD], values, low, zero, mask
        )
        return carry

    lax.fori_loop(0, GROUP_HEADS, first, 0)
    for least, slot in ((1, 1), (2, 3), (3, 2)):

        @pl.when(column >= least)
        def _(slot=slot):
            def more(h, carry):
                rows = columns(h, HEAD_ROWS)
                values = jnp.concatenate([held[slot, :, HD:], ones], axis=1)
                max_out[rows, :], sum_out[rows, :] = step(
                    q_out[rows, :], held[slot, :, :HD], values, max_out[rows, :], sum_out[rows, :]
                )
                return carry

            lax.fori_loop(0, GROUP_HEADS, more, 0)


STATE = (
    jax.ShapeDtypeStruct((ALL_ROWS, HD), jnp.float32),
    jax.ShapeDtypeStruct((ALL_ROWS, 2 * HD), jnp.float32),
)


def question_part(place, pieces, left, right, far):
    flags = jax.ShapeDtypeStruct((16 * LOCAL, HD), jnp.float32)
    return pl.pallas_call(
        question_kernel,
        out_shape=[bf16_shape(ALL_ROWS, HD), *STATE, flags],
        in_specs=[SMEM] + [VMEM] * 7,
        out_specs=[VMEM] * 4,
        scratch_shapes=[pltpu.VMEM((4, HEAD_ROWS, 2 * HD), BF16)],
        compiler_params=params(),
        cost_estimate=cost(4 * ALL_ROWS * 1024 * HD, 4 << 20),
    )(place, *pieces, left, right, far)


def passage_kernel(layout, last, flag_ref, q_ref, max_ref, sum_ref, *refs):
    tiles, refs = refs[: len(layout)], refs[len(layout) :]
    outs, value_refs = refs[: -len(layout)], refs[-len(layout) :]
    for (first, count), tile, value_ref in zip(layout, tiles, value_refs):
        tokens = tile.shape[0] // count
        value_ref[:, :HD] = tile[:, HD:]
        for block in range(count):
            flag = jnp.broadcast_to(flag_ref[first + block : first + block + 1, :], (tokens, HD))
            value_ref[block * tokens : (block + 1) * tokens, HD:] = flag.astype(BF16)

    def one(t, carry):
        rows = columns(t, STEP_ROWS)
        query, state_max, state_sum = q_ref[rows, :], max_ref[rows, :], sum_ref[rows, :]
        for tile, value_ref in zip(tiles, value_refs):
            size = tile.shape[0]
            for start in range(0, size, KEY_TILE):
                stop = min(start + KEY_TILE, size)
                state_max, state_sum = step(
                    query, tile[start:stop, :HD], value_ref[start:stop, :], state_max, state_sum
                )
        if last:
            result = (state_sum[:, :HD] / state_sum[:, HD:]).astype(BF16)
            for u in range(STEP_HEADS):
                for offset, out in enumerate(outs):
                    start = u * HEAD_ROWS + offset * ROWS
                    out[:, columns(t * STEP_HEADS + u, HD)] = result[start : start + ROWS, :]
        else:
            outs[0][rows, :] = state_max
            outs[1][rows, :] = state_sum
        return carry

    lax.fori_loop(0, GROUP_HEADS // STEP_HEADS, one, 0)


def passage_part(flags, query, state, tiles, layout, last):
    shapes = [bf16_shape(ROWS, QCOLS)] * 4 if last else list(STATE)
    keys = sum(tile.shape[0] for tile in tiles)
    return pl.pallas_call(
        functools.partial(passage_kernel, layout, last),
        out_shape=shapes,
        in_specs=[VMEM] * (4 + len(tiles)),
        out_specs=[VMEM] * len(shapes),
        scratch_shapes=[pltpu.VMEM((tile.shape[0], 2 * HD), BF16) for tile in tiles],
        compiler_params=params(),
        cost_estimate=cost(4 * ALL_ROWS * keys * HD * 2, 8 << 20),
    )(flags, query, *state, *tiles)


def join_kernel(head_ref, *refs):
    out = refs[-1]
    for offset, piece in enumerate(refs[:-1]):
        out[:, columns(head_ref[0] ^ offset, QCOLS)] = piece[...]


def join_outputs(head, pieces):
    return pl.pallas_call(
        join_kernel,
        out_shape=bf16_shape(ROWS, HQ * HD),
        in_specs=[SMEM] + [VMEM] * 4,
        out_specs=VMEM,
        compiler_params=params(16),
        cost_estimate=cost(0, 1 << 20),
    )(head, *pieces)


def swap_heads(pieces):
    moved = [pieces[0]]
    for offset in range(1, 4):
        pairs = [(i, i ^ offset) for i in range(4)]
        moved.append(lax.ppermute(pieces[offset], HEAD_AXES, pairs))
    return moved


def along(axis, value, hops):
    return lax.ppermute(value, axis, [(i, (i + hops) % 4) for i in range(4)])


def ints(*values):
    return jnp.stack([jnp.asarray(value, jnp.int32) for value in values])


def body(queries, question_kv, passage_kv, wanted, live):
    x = lax.axis_index("x")
    store = lax.axis_index("zlo") * 4 + lax.axis_index("y")
    head = lax.axis_index("zhi") * 2 + lax.axis_index("core")

    wanted_ids = wanted[:, 0, :]
    owner_ids = wanted_ids // (GROUPS * STORED)
    slots = jnp.sum(jnp.where(owner_ids == store, wanted_ids % STORED, 0), axis=1)
    slots = slots.astype(jnp.int32)

    owners = lax.dynamic_index_in_dim(owner_ids, store, 0, keepdims=True)
    count = lax.dynamic_index_in_dim(live, store, 0, keepdims=True)
    info = jnp.concatenate(
        [jnp.pad(owners, ((0, 0), (0, HD - LOCAL))), jnp.broadcast_to(count, (1, HD))], axis=1
    )
    info = jnp.broadcast_to(info.astype(BF16), (INFO_ROWS, 2 * HD))
    outgoing = select_blocks(slots, passage_kv)
    pieces = swap_heads(split_queries(ints(head), queries, question_kv, info))
    *outgoing, p1, p2, p3 = lax.optimization_barrier((*outgoing, *pieces[1:]))
    pieces = [pieces[0], p1, p2, p3]

    question, near = collect(pieces)
    owners, counts = near[:, :LOCAL], near[:, HD : HD + 1]
    offset = lax.broadcasted_iota(jnp.int32, (4, LOCAL), 0)
    slot = owners * KVH + (head ^ offset)
    read = lax.broadcasted_iota(jnp.int32, (4, LOCAL), 1) < counts
    landed_slots = jnp.where(read, slot, slot[:, :1]).reshape(-1)
    landed_flags = read.astype(jnp.int32).reshape(-1)

    query, *state, flags = question_part(
        ints(head, x),
        pieces,
        along("x", question, 1),
        along("x", question, 3),
        along("x", question, 2),
    )

    quarter, half = 4 * LOCAL, 2 * LOCAL
    for chunk, tokens in enumerate(CHUNKS):
        last = chunk == len(CHUNKS) - 1
        landed = lax.all_to_all(outgoing[chunk], SEND_AXES, 0, 0, tiled=True)
        landed, *state = lax.optimization_barrier((landed, *state))
        own = pack_blocks(landed_slots, landed_flags, landed)
        left, right = along("x", own, 1), along("x", own, 3)
        far = (along("x", left[: half * tokens], 1), along("x", right[half * tokens :], 3))
        near_layout = ((quarter, quarter), (2 * quarter, quarter))
        far_layout = ((3 * quarter, half), (3 * quarter + half, half))
        state = passage_part(flags, query, state, (own,), ((0, quarter),), False)
        if last:
            layout = near_layout + far_layout
            state = passage_part(flags, query, state, (left, right, *far), layout, True)
        else:
            state = passage_part(flags, query, state, (left, right), near_layout, False)
            state = passage_part(flags, query, state, far, far_layout, False)

    return join_outputs(ints(head), swap_heads(state))


def solution(mesh):
    fine = Mesh(mesh.devices.reshape(4, 4, 4, 2, 2), AXES)
    store, ctx = ("zlo", "y"), ("x", "zhi", "core")
    every = store + ctx
    return jax.shard_map(
        body,
        mesh=fine,
        in_specs=(
            P(every, None),
            P(every, None),
            P(every, None, None),
            P(None, ctx, None),
            P(None, ctx),
        ),
        out_specs=P(every, None),
        check_vma=False,
    )
```

```python
import functools
import math

import jax
import jax.numpy as jnp
from jax import lax
from jax.experimental import pallas as pl
from jax.experimental.pallas import tpu as pltpu
from jax.sharding import Mesh, PartitionSpec as P

HQ = 32
KVH = 4
HD = 128
GROUP_HEADS = HQ // KVH
BLK = 64
GROUPS = 16
LOCAL = 8
STORED = 8
ROWS = 64
INFO_ROWS = 16
QCOLS = GROUP_HEADS * HD
PIECE = QCOLS + 3 * HD
HEAD_ROWS = 4 * ROWS
ALL_ROWS = GROUP_HEADS * HEAD_ROWS
UNROLL = 4
EXP2_SCALE = math.log2(math.e) / math.sqrt(HD)
LOWEST = -1e30
CHUNKS = (48, 16)
KEY_TILE = 1024

AXES = ("zlo", "y", "x", "zhi", "core")
HEAD_AXES = ("zhi", "core")
SEND_AXES = ("zlo", "y", "zhi", "core")

VMEM = pl.BlockSpec(memory_space=pltpu.VMEM)
SMEM = pl.BlockSpec(memory_space=pltpu.SMEM)
BF16 = jnp.bfloat16


def params(mib=24):
    return pltpu.CompilerParams(vmem_limit_bytes=mib * 2**20)


def cost(flops, size):
    return pl.CostEstimate(flops=flops, bytes_accessed=size, transcendentals=0)


def bf16_shape(*dims):
    return jax.ShapeDtypeStruct(dims, BF16)


def columns(index, width):
    return pl.ds(pl.multiple_of(index * width, width), width)


def split_kernel(place_ref, q_ref, kv_ref, wanted_ref, live_ref, *refs):
    outs, info = refs[:4], refs[4]
    mine = pl.ds(place_ref[1], 1)
    owners = (wanted_ref[mine, :] // (GROUPS * STORED)).astype(jnp.float32)
    info[...] = jnp.broadcast_to(live_ref[mine, :].astype(jnp.float32), (ROWS, HD))
    info[:, :LOCAL] = jnp.broadcast_to(owners, (ROWS, LOCAL))
    for offset, out in enumerate(outs):
        head = place_ref[0] ^ offset
        out[:, :QCOLS] = q_ref[:, columns(head, QCOLS)]
        out[:, QCOLS : QCOLS + HD] = kv_ref[:, columns(head, HD)]
        out[:, QCOLS + HD : QCOLS + 2 * HD] = kv_ref[:, columns(KVH + head, HD)]
        out[:, QCOLS + 2 * HD :] = info[...].astype(BF16)


def split_queries(place, queries, question_kv, wanted, live):
    return pl.pallas_call(
        split_kernel,
        out_shape=[bf16_shape(ROWS, PIECE)] * 4,
        in_specs=[SMEM] + [VMEM] * 4,
        out_specs=[VMEM] * 4,
        scratch_shapes=[pltpu.VMEM((ROWS, HD), jnp.float32)],
        compiler_params=params(16),
        cost_estimate=cost(0, 1 << 20),
    )(place, queries, question_kv, wanted, live)


def select_kernel(slot_ref, stored_ref, *outs):
    def one(group, carry):
        slot = slot_ref[group]
        start = 0
        for size, out in zip(CHUNKS, outs):
            tokens = slice(start, start + size)
            for head in range(KVH):
                keys = slice(head * HD, (head + 1) * HD)
                values = slice((KVH + head) * HD, (KVH + head + 1) * HD)
                out[group * KVH + head, :, :HD] = stored_ref[slot, tokens, keys]
                out[group * KVH + head, :, HD:] = stored_ref[slot, tokens, values]
            start += size
        return carry

    lax.fori_loop(0, GROUPS, one, 0)


def select_blocks(slots, stored):
    return pl.pallas_call(
        select_kernel,
        out_shape=[bf16_shape(GROUPS * KVH, size, 2 * HD) for size in CHUNKS],
        in_specs=[SMEM, VMEM],
        out_specs=[VMEM] * len(CHUNKS),
        compiler_params=params(16),
        cost_estimate=cost(0, 3 << 20),
    )(slots, stored)


def collect_kernel(p0, p1, p2, p3, question, info):
    for offset, piece in enumerate((p0, p1, p2, p3)):
        question[offset * ROWS : (offset + 1) * ROWS, :] = piece[:, QCOLS:]
        told = piece[:INFO_ROWS, QCOLS + 2 * HD :].astype(jnp.float32)
        info[offset : offset + 1, :] = told[:1, :].astype(jnp.int32)


def collect(pieces):
    return pl.pallas_call(
        collect_kernel,
        out_shape=[bf16_shape(HEAD_ROWS, 3 * HD), jax.ShapeDtypeStruct((4, HD), jnp.int32)],
        in_specs=[VMEM] * 4,
        out_specs=[VMEM] * 2,
        compiler_params=params(16),
        cost_estimate=cost(0, 1 << 20),
    )(*pieces)


def pack_kernel(slot_ref, flag_ref, landed_ref, token_ref, out_ref):
    tokens = landed_ref.shape[1]

    def one(entry, carry):
        rows = columns(entry, tokens)
        out_ref[rows, :] = landed_ref[slot_ref[entry]]

        @pl.when(flag_ref[entry] == 0)
        def _():
            out_ref[rows, HD:] = jnp.zeros((tokens, HD), BF16)

        return carry

    lax.fori_loop(0, 4 * LOCAL, one, 0)


def pack_blocks(slots, flags, landed, token):
    tokens = landed.shape[1]
    return pl.pallas_call(
        pack_kernel,
        out_shape=bf16_shape(4 * LOCAL * tokens, 2 * HD),
        in_specs=[SMEM, SMEM, VMEM, VMEM],
        out_specs=VMEM,
        compiler_params=params(16),
        cost_estimate=cost(0, 3 << 20),
    )(slots, flags, landed, token)


def step(query, keys, values, state_max, state_sum, mask=None):
    scores = lax.dot_general(
        query, keys, (((1,), (1,)), ((), ())), preferred_element_type=jnp.float32
    )
    if mask is not None:
        scores = jnp.where(mask, scores, LOWEST)
    new_max = jnp.maximum(state_max, jnp.max(scores, axis=1, keepdims=True))
    scale = jnp.exp2((state_max - new_max) * EXP2_SCALE)
    weights = jnp.exp2((scores - new_max[:, :1]) * EXP2_SCALE).astype(jnp.bfloat16)
    summed = jnp.dot(weights, values, preferred_element_type=jnp.float32)
    return new_max, state_sum * jnp.concatenate([scale, scale], axis=1) + summed


TOKEN = jax.ShapeDtypeStruct((8, HD), jnp.float32)


def question_kernel(place_ref, p0, p1, p2, p3, left, right, far, *refs):
    q_out, max_out, sum_out, flag_out, token, held = refs
    head, column = place_ref[0], place_ref[1]
    token[...] = jnp.zeros(TOKEN.shape, jnp.float32)
    ones = jnp.ones((HEAD_ROWS, HD), BF16)
    entry = lax.broadcasted_iota(jnp.int32, (LOCAL, HD), 0).astype(jnp.float32)

    def hold(slot, offset, piece, row, start):
        held[slot, offset * ROWS : (offset + 1) * ROWS, :] = piece[
            row : row + ROWS, start : start + 2 * HD
        ]
        info = piece[row : row + INFO_ROWS, start + 2 * HD :].astype(jnp.float32)
        count = jnp.broadcast_to(info[:1, LOCAL : LOCAL + 1], (LOCAL, HD))
        first = (slot * 4 + offset) * LOCAL
        flag_out[first : first + LOCAL, :] = (entry < count).astype(jnp.float32)

    for offset, piece in enumerate((p0, p1, p2, p3)):
        hold(0, offset, piece, 0, QCOLS)
        for h in range(GROUP_HEADS):
            start = h * HEAD_ROWS + offset * ROWS
            q_out[start : start + ROWS, :] = piece[:, h * HD : (h + 1) * HD]
        for slot, other in enumerate((left, right, far)):
            hold(slot + 1, offset, other, offset * ROWS, 0)

    def positions(axis, shape):
        index = lax.broadcasted_iota(jnp.int32, shape, axis)
        return ((index // ROWS) ^ head) * ROWS + index % ROWS

    shape = (HEAD_ROWS, HEAD_ROWS)
    mask = positions(1, shape) <= positions(0, shape)
    low = jnp.full((HEAD_ROWS, HD), LOWEST, jnp.float32)
    zero = jnp.zeros((HEAD_ROWS, 2 * HD), jnp.float32)

    def first(h, carry):
        rows = columns(h, HEAD_ROWS)
        values = jnp.concatenate([held[0, :, HD:], ones], axis=1)
        max_out[rows, :], sum_out[rows, :] = step(
            q_out[rows, :], held[0, :, :HD], values, low, zero, mask
        )
        return carry

    lax.fori_loop(0, GROUP_HEADS, first, 0, unroll=2)
    for least, slot in ((1, 1), (2, 3), (3, 2)):

        @pl.when(column >= least)
        def _(slot=slot):
            def more(h, carry):
                rows = columns(h, HEAD_ROWS)
                values = jnp.concatenate([held[slot, :, HD:], ones], axis=1)
                max_out[rows, :], sum_out[rows, :] = step(
                    q_out[rows, :], held[slot, :, :HD], values, max_out[rows, :], sum_out[rows, :]
                )
                return carry

            lax.fori_loop(0, GROUP_HEADS, more, 0, unroll=2)


STATE = (
    jax.ShapeDtypeStruct((ALL_ROWS, HD), jnp.float32),
    jax.ShapeDtypeStruct((ALL_ROWS, 2 * HD), jnp.float32),
)


def question_part(place, pieces, left, right, far):
    flags = jax.ShapeDtypeStruct((16 * LOCAL, HD), jnp.float32)
    return pl.pallas_call(
        question_kernel,
        out_shape=[bf16_shape(ALL_ROWS, HD), *STATE, flags, TOKEN],
        in_specs=[SMEM] + [VMEM] * 7,
        out_specs=[VMEM] * 5,
        scratch_shapes=[pltpu.VMEM((4, HEAD_ROWS, 2 * HD), BF16)],
        compiler_params=params(),
        cost_estimate=cost(4 * ALL_ROWS * 1024 * HD, 4 << 20),
    )(place, *pieces, left, right, far)


def halves_kernel(left_ref, right_ref, token_ref, left_out, right_out):
    middle = left_out.shape[0]
    left_out[...] = left_ref[:middle, :]
    right_out[...] = right_ref[middle:, :]


def halves(left, right, token):
    return pl.pallas_call(
        halves_kernel,
        out_shape=[bf16_shape(left.shape[0] // 2, 2 * HD)] * 2,
        in_specs=[VMEM] * 3,
        out_specs=[VMEM] * 2,
        compiler_params=params(16),
        cost_estimate=cost(0, 1 << 20),
    )(left, right, token)


def passage_kernel(layout, last, flag_ref, q_ref, max_in, sum_in, *refs):
    tiles, refs = refs[: len(layout)], refs[len(layout) :]
    outs, (key_ref, value_ref) = refs[:-2], refs[-2:]
    if not last:
        outs[2][...] = jnp.zeros(TOKEN.shape, jnp.float32)
    start = 0
    for (first, blocks), tile in zip(layout, tiles):
        size = tile.shape[0]
        tokens = size // blocks
        key_ref[start : start + size, :] = tile[:, :HD]
        value_ref[start : start + size, :HD] = tile[:, HD:]
        for block in range(blocks):
            flag = jnp.broadcast_to(flag_ref[first + block : first + block + 1, :], (tokens, HD))
            rows = slice(start + block * tokens, start + (block + 1) * tokens)
            value_ref[rows, HD:] = flag.astype(BF16)
        start += size
    total = start
    parts = -(-total // KEY_TILE)
    width = total // parts

    def one(h, carry):
        rows = columns(h, HEAD_ROWS)
        query, state_max, state_sum = q_ref[rows, :], max_in[rows, :], sum_in[rows, :]
        for part in range(parts):
            keys = slice(part * width, (part + 1) * width)
            state_max, state_sum = step(
                query, key_ref[keys, :], value_ref[keys, :], state_max, state_sum
            )
        if last:
            result = (state_sum[:, :HD] / state_sum[:, HD:]).astype(BF16)
            for offset, out in enumerate(outs):
                out[:, columns(h, HD)] = result[offset * ROWS : (offset + 1) * ROWS, :]
        else:
            outs[0][rows, :] = state_max
            outs[1][rows, :] = state_sum
        return carry

    lax.fori_loop(0, GROUP_HEADS, one, 0, unroll=UNROLL)


def passage_part(flags, query, state, tiles, layout, last):
    shapes = [bf16_shape(ROWS, QCOLS)] * 4 if last else [*STATE, TOKEN]
    keys = sum(tile.shape[0] for tile in tiles)
    return pl.pallas_call(
        functools.partial(passage_kernel, layout, last),
        out_shape=shapes,
        in_specs=[VMEM] * (4 + len(tiles)),
        out_specs=[VMEM] * len(shapes),
        scratch_shapes=[
            pltpu.VMEM((keys, HD), BF16),
            pltpu.VMEM((keys, 2 * HD), BF16),
        ],
        compiler_params=params(),
        cost_estimate=cost(4 * ALL_ROWS * keys * HD * 2, 8 << 20),
    )(flags, query, *state, *tiles)


def join_kernel(head_ref, *refs):
    out = refs[-1]
    for offset, piece in enumerate(refs[:-1]):
        out[:, columns(head_ref[0] ^ offset, QCOLS)] = piece[...]


def join_outputs(head, pieces):
    return pl.pallas_call(
        join_kernel,
        out_shape=bf16_shape(ROWS, HQ * HD),
        in_specs=[SMEM] + [VMEM] * 4,
        out_specs=VMEM,
        compiler_params=params(16),
        cost_estimate=cost(0, 1 << 20),
    )(head, *pieces)


def swap_heads(pieces):
    moved = [pieces[0]]
    for offset in range(1, 4):
        pairs = [(i, i ^ offset) for i in range(4)]
        moved.append(lax.ppermute(pieces[offset], HEAD_AXES, pairs))
    return moved


def along(axis, value, hops):
    return lax.ppermute(value, axis, [(i, (i + hops) % 4) for i in range(4)])


def ints(*values):
    return jnp.stack([jnp.asarray(value, jnp.int32) for value in values])


def body(queries, question_kv, passage_kv, wanted, live):
    x = lax.axis_index("x")
    store = lax.axis_index("zlo") * 4 + lax.axis_index("y")
    head = lax.axis_index("zhi") * 2 + lax.axis_index("core")

    wanted_ids = wanted[:, 0, :]
    owner_ids = wanted_ids // (GROUPS * STORED)
    slots = jnp.sum(jnp.where(owner_ids == store, wanted_ids % STORED, 0), axis=1)
    slots = slots.astype(jnp.int32)

    split = split_queries(ints(head, store), queries, question_kv, wanted_ids, live)
    pieces = swap_heads(split)
    outgoing = select_blocks(slots, passage_kv)
    *outgoing, p1, p2, p3 = lax.optimization_barrier((*outgoing, *pieces[1:]))
    pieces = [pieces[0], p1, p2, p3]

    question, near = collect(pieces)
    owners, counts = near[:, :LOCAL], near[:, LOCAL : LOCAL + 1]
    offset = lax.broadcasted_iota(jnp.int32, (4, LOCAL), 0)
    slot = owners * KVH + (head ^ offset)
    read = lax.broadcasted_iota(jnp.int32, (4, LOCAL), 1) < counts
    landed_slots = jnp.where(read, slot, slot[:, :1]).reshape(-1)
    landed_flags = read.astype(jnp.int32).reshape(-1)

    query, *state, flags, token = question_part(
        ints(head, x),
        pieces,
        along("x", question, 1),
        along("x", question, 3),
        along("x", question, 2),
    )

    quarter, half = 4 * LOCAL, 2 * LOCAL
    own_flags, left_flags, right_flags = [(i * quarter, quarter) for i in range(3)]
    far_flags = ((3 * quarter, half), (3 * quarter + half, half))

    def fetch(chunk, token):
        landed = lax.all_to_all(outgoing[chunk], SEND_AXES, 0, 0, tiled=True)
        own = pack_blocks(landed_slots, landed_flags, landed, token)
        return own, along("x", own, 1), along("x", own, 3)

    def relay(left, right, token):
        first, second = halves(left, right, token)
        return along("x", first, 1), along("x", second, 3)

    attend = functools.partial(passage_part, flags, query)
    own, left, right = fetch(0, token)
    *state, token = attend(state, (own,), (own_flags,), False)
    far = relay(left, right, token)
    *state, token = attend(state, (left, right), (left_flags, right_flags), False)
    own, left, right = fetch(1, token)
    *state, token = attend(state, far, far_flags, False)
    far = relay(left, right, token)
    layout = (own_flags, left_flags, right_flags)
    *state, token = attend(state, (own, left, right), layout, False)
    state = attend(state, far, far_flags, True)

    return join_outputs(ints(head), swap_heads(state))


def solution(mesh):
    fine = Mesh(mesh.devices.reshape(4, 4, 4, 2, 2), AXES)
    store, ctx = ("zlo", "y"), ("x", "zhi", "core")
    every = store + ctx
    return jax.shard_map(
        body,
        mesh=fine,
        in_specs=(
            P(every, None),
            P(every, None),
            P(every, None, None),
            P(None, ctx, None),
            P(None, ctx),
        ),
        out_specs=P(every, None),
        check_vma=False,
    )
```

```python
import functools
import math

import jax
import jax.numpy as jnp
from jax import lax
from jax.experimental import pallas as pl
from jax.experimental.pallas import tpu as pltpu
from jax.sharding import Mesh, PartitionSpec as P

HQ = 32
KVH = 4
HD = 128
GROUP_HEADS = HQ // KVH
BLK = 64
GROUPS = 16
LOCAL = 8
STORED = 8
ROWS = 64
INFO_ROWS = 16
QCOLS = GROUP_HEADS * HD
PIECE = QCOLS + 3 * HD
HEAD_ROWS = 4 * ROWS
ALL_ROWS = GROUP_HEADS * HEAD_ROWS
UNROLL = 4
EXP2_SCALE = math.log2(math.e) / math.sqrt(HD)
LOWEST = -1e30
CHUNKS = (64,)
KEY_TILE = 1024

AXES = ("zlo", "y", "x", "zhi", "core")
HEAD_AXES = ("zhi", "core")
SEND_AXES = ("zlo", "y", "zhi", "core")

VMEM = pl.BlockSpec(memory_space=pltpu.VMEM)
SMEM = pl.BlockSpec(memory_space=pltpu.SMEM)
BF16 = jnp.bfloat16


def params(mib=24):
    return pltpu.CompilerParams(vmem_limit_bytes=mib * 2**20)


def cost(flops, size):
    return pl.CostEstimate(flops=flops, bytes_accessed=size, transcendentals=0)


def bf16_shape(*dims):
    return jax.ShapeDtypeStruct(dims, BF16)


def columns(index, width):
    return pl.ds(pl.multiple_of(index * width, width), width)


def split_kernel(place_ref, q_ref, kv_ref, wanted_ref, live_ref, *refs):
    outs, info = refs[:4], refs[4]
    mine = pl.ds(place_ref[1], 1)
    owners = (wanted_ref[mine, :] // (GROUPS * STORED)).astype(jnp.float32)
    info[...] = jnp.broadcast_to(live_ref[mine, :].astype(jnp.float32), (ROWS, HD))
    info[:, :LOCAL] = jnp.broadcast_to(owners, (ROWS, LOCAL))
    for offset, out in enumerate(outs):
        head = place_ref[0] ^ offset
        out[:, :QCOLS] = q_ref[:, columns(head, QCOLS)]
        out[:, QCOLS : QCOLS + HD] = kv_ref[:, columns(head, HD)]
        out[:, QCOLS + HD : QCOLS + 2 * HD] = kv_ref[:, columns(KVH + head, HD)]
        out[:, QCOLS + 2 * HD :] = info[...].astype(BF16)


def split_queries(place, queries, question_kv, wanted, live):
    return pl.pallas_call(
        split_kernel,
        out_shape=[bf16_shape(ROWS, PIECE)] * 4,
        in_specs=[SMEM] + [VMEM] * 4,
        out_specs=[VMEM] * 4,
        scratch_shapes=[pltpu.VMEM((ROWS, HD), jnp.float32)],
        compiler_params=params(16),
        cost_estimate=cost(0, 1 << 20),
    )(place, queries, question_kv, wanted, live)


def select_kernel(slot_ref, stored_ref, *outs):
    def one(group, carry):
        slot = slot_ref[group]
        start = 0
        for size, out in zip(CHUNKS, outs):
            tokens = slice(start, start + size)
            for head in range(KVH):
                keys = slice(head * HD, (head + 1) * HD)
                values = slice((KVH + head) * HD, (KVH + head + 1) * HD)
                out[group * KVH + head, :, :HD] = stored_ref[slot, tokens, keys]
                out[group * KVH + head, :, HD:] = stored_ref[slot, tokens, values]
            start += size
        return carry

    lax.fori_loop(0, GROUPS, one, 0)


def select_blocks(slots, stored):
    return pl.pallas_call(
        select_kernel,
        out_shape=[bf16_shape(GROUPS * KVH, size, 2 * HD) for size in CHUNKS],
        in_specs=[SMEM, VMEM],
        out_specs=[VMEM] * len(CHUNKS),
        compiler_params=params(16),
        cost_estimate=cost(0, 3 << 20),
    )(slots, stored)


def collect_kernel(p0, p1, p2, p3, question, info):
    for offset, piece in enumerate((p0, p1, p2, p3)):
        question[offset * ROWS : (offset + 1) * ROWS, :] = piece[:, QCOLS:]
        told = piece[:INFO_ROWS, QCOLS + 2 * HD :].astype(jnp.float32)
        info[offset : offset + 1, :] = told[:1, :].astype(jnp.int32)


def collect(pieces):
    return pl.pallas_call(
        collect_kernel,
        out_shape=[bf16_shape(HEAD_ROWS, 3 * HD), jax.ShapeDtypeStruct((4, HD), jnp.int32)],
        in_specs=[VMEM] * 4,
        out_specs=[VMEM] * 2,
        compiler_params=params(16),
        cost_estimate=cost(0, 1 << 20),
    )(*pieces)


def pack_kernel(slot_ref, flag_ref, landed_ref, token_ref, *outs):
    tokens = landed_ref.shape[1]
    for part, out in enumerate(outs):

        def one(place, carry, part=part, out=out):
            entry = part * 2 * LOCAL + place
            rows = columns(place, tokens)
            out[rows, :] = landed_ref[slot_ref[entry]]

            @pl.when(flag_ref[entry] == 0)
            def _():
                out[rows, HD:] = jnp.zeros((tokens, HD), BF16)

            return carry

        lax.fori_loop(0, 2 * LOCAL, one, 0)


def pack_blocks(slots, flags, landed, token):
    tokens = landed.shape[1]
    return pl.pallas_call(
        pack_kernel,
        out_shape=[bf16_shape(2 * LOCAL * tokens, 2 * HD)] * 2,
        in_specs=[SMEM, SMEM, VMEM, VMEM],
        out_specs=[VMEM] * 2,
        compiler_params=params(16),
        cost_estimate=cost(0, 3 << 20),
    )(slots, flags, landed, token)


def step(query, keys, values, state_max, state_sum, mask=None):
    scores = lax.dot_general(
        query, keys, (((1,), (1,)), ((), ())), preferred_element_type=jnp.float32
    )
    if mask is not None:
        scores = jnp.where(mask, scores, LOWEST)
    new_max = jnp.maximum(state_max, jnp.max(scores, axis=1, keepdims=True))
    scale = jnp.exp2((state_max - new_max) * EXP2_SCALE)
    weights = jnp.exp2((scores - new_max[:, :1]) * EXP2_SCALE).astype(jnp.bfloat16)
    summed = jnp.dot(weights, values, preferred_element_type=jnp.float32)
    return new_max, state_sum * jnp.concatenate([scale, scale], axis=1) + summed


TOKEN = jax.ShapeDtypeStruct((8, HD), jnp.float32)


def question_kernel(place_ref, p0, p1, p2, p3, left, right, far, *refs):
    q_out, max_out, sum_out, flag_out, token, held = refs
    head, column = place_ref[0], place_ref[1]
    token[...] = jnp.zeros(TOKEN.shape, jnp.float32)
    ones = jnp.ones((HEAD_ROWS, HD), BF16)
    entry = lax.broadcasted_iota(jnp.int32, (LOCAL, HD), 0).astype(jnp.float32)

    def hold(slot, offset, piece, row, start):
        held[slot, offset * ROWS : (offset + 1) * ROWS, :] = piece[
            row : row + ROWS, start : start + 2 * HD
        ]
        info = piece[row : row + INFO_ROWS, start + 2 * HD :].astype(jnp.float32)
        count = jnp.broadcast_to(info[:1, LOCAL : LOCAL + 1], (LOCAL, HD))
        first = (slot * 4 + offset) * LOCAL
        flag_out[first : first + LOCAL, :] = (entry < count).astype(jnp.float32)

    for offset, piece in enumerate((p0, p1, p2, p3)):
        hold(0, offset, piece, 0, QCOLS)
        for h in range(GROUP_HEADS):
            start = h * HEAD_ROWS + offset * ROWS
            q_out[start : start + ROWS, :] = piece[:, h * HD : (h + 1) * HD]
        for slot, other in enumerate((left, right, far)):
            hold(slot + 1, offset, other, offset * ROWS, 0)

    def positions(axis, shape):
        index = lax.broadcasted_iota(jnp.int32, shape, axis)
        return ((index // ROWS) ^ head) * ROWS + index % ROWS

    shape = (HEAD_ROWS, HEAD_ROWS)
    mask = positions(1, shape) <= positions(0, shape)
    low = jnp.full((HEAD_ROWS, HD), LOWEST, jnp.float32)
    zero = jnp.zeros((HEAD_ROWS, 2 * HD), jnp.float32)

    def first(h, carry):
        rows = columns(h, HEAD_ROWS)
        values = jnp.concatenate([held[0, :, HD:], ones], axis=1)
        max_out[rows, :], sum_out[rows, :] = step(
            q_out[rows, :], held[0, :, :HD], values, low, zero, mask
        )
        return carry

    lax.fori_loop(0, GROUP_HEADS, first, 0, unroll=2)
    for least, slot in ((1, 1), (2, 3), (3, 2)):

        @pl.when(column >= least)
        def _(slot=slot):
            def more(h, carry):
                rows = columns(h, HEAD_ROWS)
                values = jnp.concatenate([held[slot, :, HD:], ones], axis=1)
                max_out[rows, :], sum_out[rows, :] = step(
                    q_out[rows, :], held[slot, :, :HD], values, max_out[rows, :], sum_out[rows, :]
                )
                return carry

            lax.fori_loop(0, GROUP_HEADS, more, 0, unroll=2)


STATE = (
    jax.ShapeDtypeStruct((ALL_ROWS, HD), jnp.float32),
    jax.ShapeDtypeStruct((ALL_ROWS, 2 * HD), jnp.float32),
)


def question_part(place, pieces, left, right, far):
    flags = jax.ShapeDtypeStruct((16 * LOCAL, HD), jnp.float32)
    return pl.pallas_call(
        question_kernel,
        out_shape=[bf16_shape(ALL_ROWS, HD), *STATE, flags, TOKEN],
        in_specs=[SMEM] + [VMEM] * 7,
        out_specs=[VMEM] * 5,
        scratch_shapes=[pltpu.VMEM((4, HEAD_ROWS, 2 * HD), BF16)],
        compiler_params=params(),
        cost_estimate=cost(4 * ALL_ROWS * 1024 * HD, 4 << 20),
    )(place, *pieces, left, right, far)


def passage_kernel(layout, last, flag_ref, q_ref, max_in, sum_in, *refs):
    tiles, refs = refs[: len(layout)], refs[len(layout) :]
    outs, (key_ref, value_ref) = refs[:-2], refs[-2:]
    if not last:
        outs[2][...] = jnp.zeros(TOKEN.shape, jnp.float32)
    start = 0
    for (first, blocks), tile in zip(layout, tiles):
        size = tile.shape[0]
        tokens = size // blocks
        key_ref[start : start + size, :] = tile[:, :HD]
        value_ref[start : start + size, :HD] = tile[:, HD:]
        for block in range(blocks):
            flag = jnp.broadcast_to(flag_ref[first + block : first + block + 1, :], (tokens, HD))
            rows = slice(start + block * tokens, start + (block + 1) * tokens)
            value_ref[rows, HD:] = flag.astype(BF16)
        start += size
    total = start
    parts = -(-total // KEY_TILE)
    width = total // parts

    def one(h, carry):
        rows = columns(h, HEAD_ROWS)
        query, state_max, state_sum = q_ref[rows, :], max_in[rows, :], sum_in[rows, :]
        for part in range(parts):
            keys = slice(part * width, (part + 1) * width)
            state_max, state_sum = step(
                query, key_ref[keys, :], value_ref[keys, :], state_max, state_sum
            )
        if last:
            result = (state_sum[:, :HD] / state_sum[:, HD:]).astype(BF16)
            for offset, out in enumerate(outs):
                out[:, columns(h, HD)] = result[offset * ROWS : (offset + 1) * ROWS, :]
        else:
            outs[0][rows, :] = state_max
            outs[1][rows, :] = state_sum
        return carry

    lax.fori_loop(0, GROUP_HEADS, one, 0, unroll=UNROLL)


def passage_part(flags, query, state, tiles, layout, last):
    shapes = [bf16_shape(ROWS, QCOLS)] * 4 if last else [*STATE, TOKEN]
    keys = sum(tile.shape[0] for tile in tiles)
    return pl.pallas_call(
        functools.partial(passage_kernel, layout, last),
        out_shape=shapes,
        in_specs=[VMEM] * (4 + len(tiles)),
        out_specs=[VMEM] * len(shapes),
        scratch_shapes=[
            pltpu.VMEM((keys, HD), BF16),
            pltpu.VMEM((keys, 2 * HD), BF16),
        ],
        compiler_params=params(),
        cost_estimate=cost(4 * ALL_ROWS * keys * HD * 2, 8 << 20),
    )(flags, query, *state, *tiles)


def join_kernel(head_ref, *refs):
    out = refs[-1]
    for offset, piece in enumerate(refs[:-1]):
        out[:, columns(head_ref[0] ^ offset, QCOLS)] = piece[...]


def join_outputs(head, pieces):
    return pl.pallas_call(
        join_kernel,
        out_shape=bf16_shape(ROWS, HQ * HD),
        in_specs=[SMEM] + [VMEM] * 4,
        out_specs=VMEM,
        compiler_params=params(16),
        cost_estimate=cost(0, 1 << 20),
    )(head, *pieces)


def swap_heads(pieces):
    moved = [pieces[0]]
    for offset in range(1, 4):
        pairs = [(i, i ^ offset) for i in range(4)]
        moved.append(lax.ppermute(pieces[offset], HEAD_AXES, pairs))
    return moved


def along(axis, value, hops):
    return lax.ppermute(value, axis, [(i, (i + hops) % 4) for i in range(4)])


def ints(*values):
    return jnp.stack([jnp.asarray(value, jnp.int32) for value in values])


def body(queries, question_kv, passage_kv, wanted, live):
    x = lax.axis_index("x")
    store = lax.axis_index("zlo") * 4 + lax.axis_index("y")
    head = lax.axis_index("zhi") * 2 + lax.axis_index("core")

    wanted_ids = wanted[:, 0, :]
    owner_ids = wanted_ids // (GROUPS * STORED)
    slots = jnp.sum(jnp.where(owner_ids == store, wanted_ids % STORED, 0), axis=1)
    slots = slots.astype(jnp.int32)

    split = split_queries(ints(head, store), queries, question_kv, wanted_ids, live)
    pieces = swap_heads(split)
    outgoing = select_blocks(slots, passage_kv)
    *outgoing, p1, p2, p3 = lax.optimization_barrier((*outgoing, *pieces[1:]))
    pieces = [pieces[0], p1, p2, p3]

    question, near = collect(pieces)
    owners, counts = near[:, :LOCAL], near[:, LOCAL : LOCAL + 1]
    offset = lax.broadcasted_iota(jnp.int32, (4, LOCAL), 0)
    slot = owners * KVH + (head ^ offset)
    read = lax.broadcasted_iota(jnp.int32, (4, LOCAL), 1) < counts
    landed_slots = jnp.where(read, slot, slot[:, :1]).reshape(-1)
    landed_flags = read.astype(jnp.int32).reshape(-1)

    query, *state, flags, token = question_part(
        ints(head, x),
        pieces,
        along("x", question, 1),
        along("x", question, 3),
        along("x", question, 2),
    )

    landed = lax.all_to_all(outgoing[0], SEND_AXES, 0, 0, tiled=True)
    own_a, own_b = pack_blocks(landed_slots, landed_flags, landed, token)
    left_a, right_b = along("x", own_a, 1), along("x", own_b, 3)
    left_b, right_a = along("x", own_b, 1), along("x", own_a, 3)

    half = 2 * LOCAL
    layouts = [((i * half, half), (j * half, half)) for i, j in ((0, 1), (2, 5), (3, 4), (6, 7))]
    attend = functools.partial(passage_part, flags, query)
    *state, _ = attend(state, (own_a, own_b), layouts[0], False)
    left_a, right_b, *state = lax.optimization_barrier((left_a, right_b, *state))
    far_a, far_b = along("x", left_a, 1), along("x", right_b, 3)
    *state, _ = attend(state, (left_a, right_b), layouts[1], False)
    *state, _ = attend(state, (left_b, right_a), layouts[2], False)
    state = attend(state, (far_a, far_b), layouts[3], True)

    return join_outputs(ints(head), swap_heads(state))


def solution(mesh):
    fine = Mesh(mesh.devices.reshape(4, 4, 4, 2, 2), AXES)
    store, ctx = ("zlo", "y"), ("x", "zhi", "core")
    every = store + ctx
    return jax.shard_map(
        body,
        mesh=fine,
        in_specs=(
            P(every, None),
            P(every, None),
            P(every, None, None),
            P(None, ctx, None),
            P(None, ctx),
        ),
        out_specs=P(every, None),
        check_vma=False,
    )
```

```python
import functools
import math

import jax
import jax.numpy as jnp
from jax import lax
from jax.experimental import pallas as pl
from jax.experimental.pallas import tpu as pltpu
from jax.sharding import Mesh, PartitionSpec as P

HQ = 32
KVH = 4
HD = 128
GROUP_HEADS = HQ // KVH
BLK = 64
GROUPS = 16
LOCAL = 8
STORED = 8
ROWS = 64
INFO_ROWS = 16
QCOLS = GROUP_HEADS * HD
PIECE = QCOLS + 3 * HD
HEAD_ROWS = 4 * ROWS
ALL_ROWS = GROUP_HEADS * HEAD_ROWS
UNROLL = 8
EXP2_SCALE = math.log2(math.e) / math.sqrt(HD)
LOWEST = -1e30
CHUNKS = (64,)
KEY_TILE = 1024

AXES = ("zlo", "y", "x", "zhi", "core")
HEAD_AXES = ("zhi", "core")
SEND_AXES = ("zlo", "y", "zhi", "core")

VMEM = pl.BlockSpec(memory_space=pltpu.VMEM)
SMEM = pl.BlockSpec(memory_space=pltpu.SMEM)
BF16 = jnp.bfloat16


def params(mib=24):
    return pltpu.CompilerParams(vmem_limit_bytes=mib * 2**20)


def cost(flops, size):
    return pl.CostEstimate(flops=flops, bytes_accessed=size, transcendentals=0)


def bf16_shape(*dims):
    return jax.ShapeDtypeStruct(dims, BF16)


def columns(index, width):
    return pl.ds(pl.multiple_of(index * width, width), width)


def split_kernel(place_ref, q_ref, kv_ref, lists_ref, *refs):
    outs, sems = refs[:4], refs[4]
    copies = []
    for offset, out in enumerate(outs):
        head = place_ref[0] ^ offset
        moves = (
            (q_ref.at[:, columns(head, QCOLS)], 0, QCOLS),
            (kv_ref.at[:, columns(head, HD)], QCOLS, HD),
            (kv_ref.at[:, columns(KVH + head, HD)], QCOLS + HD, HD),
        )
        for index, (source, start, width) in enumerate(moves):
            target = out.at[:, start : start + width]
            copies.append(pltpu.make_async_copy(source, target, sems.at[offset, index]))
    for copy in copies:
        copy.start()
    lists = lists_ref[pl.ds(place_ref[1], 1), :]
    told = jnp.broadcast_to(lists.astype(jnp.float32).astype(BF16), (ROWS, HD))
    for out in outs:
        out[:, QCOLS + 2 * HD :] = told
    for copy in copies:
        copy.wait()


def split_queries(place, queries, question_kv, lists):
    queries = pltpu.with_memory_space_constraint(queries, pltpu.HBM)
    question_kv = pltpu.with_memory_space_constraint(question_kv, pltpu.HBM)
    hbm = pl.BlockSpec(memory_space=pltpu.HBM)
    return pl.pallas_call(
        split_kernel,
        out_shape=[bf16_shape(ROWS, PIECE)] * 4,
        in_specs=[SMEM, hbm, hbm, VMEM],
        out_specs=[VMEM] * 4,
        scratch_shapes=[pltpu.SemaphoreType.DMA((4, 3))],
        compiler_params=params(16),
        cost_estimate=cost(0, 1 << 20),
    )(place, queries, question_kv, lists)


def select_kernel(slot_ref, stored_ref, *outs):
    def one(group, carry):
        slot = slot_ref[group]
        start = 0
        for size, out in zip(CHUNKS, outs):
            tokens = slice(start, start + size)
            for head in range(KVH):
                keys = slice(head * HD, (head + 1) * HD)
                values = slice((KVH + head) * HD, (KVH + head + 1) * HD)
                out[group * KVH + head, :, :HD] = stored_ref[slot, tokens, keys]
                out[group * KVH + head, :, HD:] = stored_ref[slot, tokens, values]
            start += size
        return carry

    lax.fori_loop(0, GROUPS, one, 0)


def select_blocks(slots, stored):
    return pl.pallas_call(
        select_kernel,
        out_shape=[bf16_shape(GROUPS * KVH, size, 2 * HD) for size in CHUNKS],
        in_specs=[SMEM, VMEM],
        out_specs=[VMEM] * len(CHUNKS),
        compiler_params=params(16),
        cost_estimate=cost(0, 3 << 20),
    )(slots, stored)


def collect_kernel(p0, p1, p2, p3, question, info):
    for offset, piece in enumerate((p0, p1, p2, p3)):
        question[offset * ROWS : (offset + 1) * ROWS, :] = piece[:, QCOLS:]
        told = piece[:INFO_ROWS, QCOLS + 2 * HD :].astype(jnp.float32)
        info[offset : offset + 1, :] = told[:1, :].astype(jnp.int32)


def collect(pieces):
    return pl.pallas_call(
        collect_kernel,
        out_shape=[bf16_shape(HEAD_ROWS, 3 * HD), jax.ShapeDtypeStruct((4, HD), jnp.int32)],
        in_specs=[VMEM] * 4,
        out_specs=[VMEM] * 2,
        compiler_params=params(16),
        cost_estimate=cost(0, 1 << 20),
    )(*pieces)


def pack_kernel(slot_ref, flag_ref, landed_ref, token_ref, *outs):
    tokens = landed_ref.shape[1]
    for part, out in enumerate(outs):

        def one(place, carry, part=part, out=out):
            entry = part * 2 * LOCAL + place
            rows = columns(place, tokens)
            out[rows, :] = landed_ref[slot_ref[entry]]

            @pl.when(flag_ref[entry] == 0)
            def _():
                out[rows, HD:] = jnp.zeros((tokens, HD), BF16)

            return carry

        lax.fori_loop(0, 2 * LOCAL, one, 0)


def pack_blocks(slots, flags, landed, token):
    tokens = landed.shape[1]
    return pl.pallas_call(
        pack_kernel,
        out_shape=[bf16_shape(2 * LOCAL * tokens, 2 * HD)] * 2,
        in_specs=[SMEM, SMEM, VMEM, VMEM],
        out_specs=[VMEM] * 2,
        compiler_params=params(16),
        cost_estimate=cost(0, 3 << 20),
    )(slots, flags, landed, token)


def step(query, keys, values, state_max, state_sum, mask=None):
    scores = lax.dot_general(
        query, keys, (((1,), (1,)), ((), ())), preferred_element_type=jnp.float32
    )
    if mask is not None:
        scores = jnp.where(mask, scores, LOWEST)
    new_max = jnp.maximum(state_max, jnp.max(scores, axis=1, keepdims=True))
    scale = jnp.exp2((state_max - new_max) * EXP2_SCALE)
    weights = jnp.exp2((scores - new_max[:, :1]) * EXP2_SCALE).astype(jnp.bfloat16)
    summed = jnp.dot(weights, values, preferred_element_type=jnp.float32)
    return new_max, state_sum * jnp.concatenate([scale, scale], axis=1) + summed


TOKEN = jax.ShapeDtypeStruct((8, HD), jnp.float32)


def question_kernel(place_ref, p0, p1, p2, p3, left, right, far, *refs):
    q_out, max_out, sum_out, flag_out, token, held = refs
    head, column = place_ref[0], place_ref[1]
    token[...] = jnp.zeros(TOKEN.shape, jnp.float32)
    ones = jnp.ones((HEAD_ROWS, HD), BF16)
    entry = lax.broadcasted_iota(jnp.int32, (LOCAL, HD), 0).astype(jnp.float32)

    def hold(slot, offset, piece, row, start):
        held[slot, offset * ROWS : (offset + 1) * ROWS, :] = piece[
            row : row + ROWS, start : start + 2 * HD
        ]
        info = piece[row : row + INFO_ROWS, start + 2 * HD :].astype(jnp.float32)
        count = jnp.broadcast_to(info[:1, LOCAL : LOCAL + 1], (LOCAL, HD))
        first = (slot * 4 + offset) * LOCAL
        flag_out[first : first + LOCAL, :] = (entry < count).astype(jnp.float32)

    for offset, piece in enumerate((p0, p1, p2, p3)):
        hold(0, offset, piece, 0, QCOLS)
        for h in range(GROUP_HEADS):
            start = h * HEAD_ROWS + offset * ROWS
            q_out[start : start + ROWS, :] = piece[:, h * HD : (h + 1) * HD]
        for slot, other in enumerate((left, right, far)):
            hold(slot + 1, offset, other, offset * ROWS, 0)

    def positions(axis, shape):
        index = lax.broadcasted_iota(jnp.int32, shape, axis)
        return ((index // ROWS) ^ head) * ROWS + index % ROWS

    shape = (HEAD_ROWS, HEAD_ROWS)
    mask = positions(1, shape) <= positions(0, shape)
    low = jnp.full((HEAD_ROWS, HD), LOWEST, jnp.float32)
    zero = jnp.zeros((HEAD_ROWS, 2 * HD), jnp.float32)

    def first(h, carry):
        rows = columns(h, HEAD_ROWS)
        values = jnp.concatenate([held[0, :, HD:], ones], axis=1)
        max_out[rows, :], sum_out[rows, :] = step(
            q_out[rows, :], held[0, :, :HD], values, low, zero, mask
        )
        return carry

    lax.fori_loop(0, GROUP_HEADS, first, 0, unroll=2)
    for least, slot in ((1, 1), (2, 3), (3, 2)):

        @pl.when(column >= least)
        def _(slot=slot):
            def more(h, carry):
                rows = columns(h, HEAD_ROWS)
                values = jnp.concatenate([held[slot, :, HD:], ones], axis=1)
                max_out[rows, :], sum_out[rows, :] = step(
                    q_out[rows, :], held[slot, :, :HD], values, max_out[rows, :], sum_out[rows, :]
                )
                return carry

            lax.fori_loop(0, GROUP_HEADS, more, 0, unroll=2)


STATE = (
    jax.ShapeDtypeStruct((ALL_ROWS, HD), jnp.float32),
    jax.ShapeDtypeStruct((ALL_ROWS, 2 * HD), jnp.float32),
)


def question_part(place, pieces, left, right, far):
    flags = jax.ShapeDtypeStruct((16 * LOCAL, HD), jnp.float32)
    return pl.pallas_call(
        question_kernel,
        out_shape=[bf16_shape(ALL_ROWS, HD), *STATE, flags, TOKEN],
        in_specs=[SMEM] + [VMEM] * 7,
        out_specs=[VMEM] * 5,
        scratch_shapes=[pltpu.VMEM((4, HEAD_ROWS, 2 * HD), BF16)],
        compiler_params=params(),
        cost_estimate=cost(4 * ALL_ROWS * 1024 * HD, 4 << 20),
    )(place, *pieces, left, right, far)


def passage_kernel(layout, last, flag_ref, q_ref, max_in, sum_in, *refs):
    tiles, refs = refs[: len(layout)], refs[len(layout) :]
    outs, (key_ref, value_ref) = refs[:-2], refs[-2:]
    if not last:
        outs[2][...] = jnp.zeros(TOKEN.shape, jnp.float32)
    start = 0
    for (first, blocks), tile in zip(layout, tiles):
        size = tile.shape[0]
        tokens = size // blocks
        key_ref[start : start + size, :] = tile[:, :HD]
        value_ref[start : start + size, :HD] = tile[:, HD:]
        for block in range(blocks):
            flag = jnp.broadcast_to(flag_ref[first + block : first + block + 1, :], (tokens, HD))
            rows = slice(start + block * tokens, start + (block + 1) * tokens)
            value_ref[rows, HD:] = flag.astype(BF16)
        start += size
    total = start
    parts = -(-total // KEY_TILE)
    width = total // parts

    def one(h, carry):
        rows = columns(h, HEAD_ROWS)
        query, state_max, state_sum = q_ref[rows, :], max_in[rows, :], sum_in[rows, :]
        for part in range(parts):
            keys = slice(part * width, (part + 1) * width)
            state_max, state_sum = step(
                query, key_ref[keys, :], value_ref[keys, :], state_max, state_sum
            )
        if last:
            result = (state_sum[:, :HD] / state_sum[:, HD:]).astype(BF16)
            for offset, out in enumerate(outs):
                out[:, columns(h, HD)] = result[offset * ROWS : (offset + 1) * ROWS, :]
        else:
            outs[0][rows, :] = state_max
            outs[1][rows, :] = state_sum
        return carry

    lax.fori_loop(0, GROUP_HEADS, one, 0, unroll=UNROLL)


def passage_part(flags, query, state, tiles, layout, last):
    shapes = [bf16_shape(ROWS, QCOLS)] * 4 if last else [*STATE, TOKEN]
    keys = sum(tile.shape[0] for tile in tiles)
    return pl.pallas_call(
        functools.partial(passage_kernel, layout, last),
        out_shape=shapes,
        in_specs=[VMEM] * (4 + len(tiles)),
        out_specs=[VMEM] * len(shapes),
        scratch_shapes=[
            pltpu.VMEM((keys, HD), BF16),
            pltpu.VMEM((keys, 2 * HD), BF16),
        ],
        compiler_params=params(),
        cost_estimate=cost(4 * ALL_ROWS * keys * HD * 2, 8 << 20),
    )(flags, query, *state, *tiles)


def join_kernel(head_ref, *refs):
    out = refs[-1]
    for offset, piece in enumerate(refs[:-1]):
        out[:, columns(head_ref[0] ^ offset, QCOLS)] = piece[...]


def join_outputs(head, pieces):
    return pl.pallas_call(
        join_kernel,
        out_shape=bf16_shape(ROWS, HQ * HD),
        in_specs=[SMEM] + [VMEM] * 4,
        out_specs=VMEM,
        compiler_params=params(16),
        cost_estimate=cost(0, 1 << 20),
    )(head, *pieces)


def swap_heads(pieces):
    moved = [pieces[0]]
    for offset in range(1, 4):
        pairs = [(i, i ^ offset) for i in range(4)]
        moved.append(lax.ppermute(pieces[offset], HEAD_AXES, pairs))
    return moved


def along(axis, value, hops):
    return lax.ppermute(value, axis, [(i, (i + hops) % 4) for i in range(4)])


def ints(*values):
    return jnp.stack([jnp.asarray(value, jnp.int32) for value in values])


def body(queries, question_kv, passage_kv, wanted, live):
    x = lax.axis_index("x")
    store = lax.axis_index("zlo") * 4 + lax.axis_index("y")
    head = lax.axis_index("zhi") * 2 + lax.axis_index("core")

    wanted_ids = wanted[:, 0, :]
    owner_ids = wanted_ids // (GROUPS * STORED)
    slots = jnp.sum(jnp.where(owner_ids == store, wanted_ids % STORED, 0), axis=1)
    slots = slots.astype(jnp.int32)

    lists = jnp.concatenate(
        [owner_ids, live, jnp.zeros((GROUPS, HD - LOCAL - 1), jnp.int32)], axis=1
    )
    split = split_queries(ints(head, store), queries, question_kv, lists)
    pieces = swap_heads(split)
    outgoing = select_blocks(slots, passage_kv)
    *outgoing, p1, p2, p3 = lax.optimization_barrier((*outgoing, *pieces[1:]))
    pieces = [pieces[0], p1, p2, p3]

    question, near = collect(pieces)
    owners, counts = near[:, :LOCAL], near[:, LOCAL : LOCAL + 1]
    offset = lax.broadcasted_iota(jnp.int32, (4, LOCAL), 0)
    slot = owners * KVH + (head ^ offset)
    read = lax.broadcasted_iota(jnp.int32, (4, LOCAL), 1) < counts
    landed_slots = jnp.where(read, slot, slot[:, :1]).reshape(-1)
    landed_flags = read.astype(jnp.int32).reshape(-1)

    query, *state, flags, token = question_part(
        ints(head, x),
        pieces,
        along("x", question, 1),
        along("x", question, 3),
        along("x", question, 2),
    )

    landed = lax.all_to_all(outgoing[0], SEND_AXES, 0, 0, tiled=True)
    own_a, own_b = pack_blocks(landed_slots, landed_flags, landed, token)
    left_a, right_b = along("x", own_a, 1), along("x", own_b, 3)
    left_b, right_a = along("x", own_b, 1), along("x", own_a, 3)

    half = 2 * LOCAL
    layouts = [((i * half, half), (j * half, half)) for i, j in ((0, 1), (2, 5), (3, 4), (6, 7))]
    attend = functools.partial(passage_part, flags, query)
    *state, _ = attend(state, (own_a, own_b), layouts[0], False)
    left_a, right_b, *state = lax.optimization_barrier((left_a, right_b, *state))
    far_a, far_b = along("x", left_a, 1), along("x", right_b, 3)
    *state, _ = attend(state, (left_a, right_b), layouts[1], False)
    *state, _ = attend(state, (left_b, right_a), layouts[2], False)
    state = attend(state, (far_a, far_b), layouts[3], True)

    return join_outputs(ints(head), swap_heads(state))


def solution(mesh):
    fine = Mesh(mesh.devices.reshape(4, 4, 4, 2, 2), AXES)
    store, ctx = ("zlo", "y"), ("x", "zhi", "core")
    every = store + ctx
    return jax.shard_map(
        body,
        mesh=fine,
        in_specs=(
            P(every, None),
            P(every, None),
            P(every, None, None),
            P(None, ctx, None),
            P(None, ctx),
        ),
        out_specs=P(every, None),
        check_vma=False,
    )
```
